512 devices in a mesh: city: 16 (over x, y), tile: 32 (over z, core).
Axes of the slice: x: 4, y: 4, z: 16, core: 2. Of those that a mesh axis runs over, the one named last changes fastest.
Arguments:
- right_side: float32 [2, 1048576], P(None, ('city', 'tile')), may hold values from -25 to 25
- noise_var: float32 [1048576], P(('city', 'tile')), may hold values from 0.1 to 1
- coords: float32 [2, 1048576], P(None, 'city'), may hold values from 0 to 641
- counts: int32 [512], P(('city', 'tile')), may hold values from 1024 to 2048
- pair_list: int32 [512, 5, 3], P(('city', 'tile')), may hold values from 0 to 31, as said below
Outputs:
- solution_field: float32 [2, 1048576], P(None, ('city', 'tile'))
- residual: float32 [2, 1048576], P(None, ('city', 'tile'))
The draws below stay inside these ranges and needn't reach their ends.
Inputs may be any that keep to these rules, and one draw needn't show every extreme that they name: `pair_list`: columns are first tile, second tile (both indices within a city) and kind: 0 an empty slot (tiles 0), 1 both tiles in the owner's city, 2 the second tile in the next city, 3 the second tile in the previous city. Every unordered pair of tiles of a city that is listed appears once in that city (a tile with itself too); a pair (a, b) of kind 2 in city c appears as (b, a) of kind 3 in city c + 1. A city lists at most 65 live pairs, at most one of kind 2 and one of kind 3. A device holds at most 5 live pairs, and some device holds that many. A tile is the first tile of, or the second tile of a kind 1 pair with a != b, in at most 3 live pairs of its city, and some tile of every city in exactly 3.
All inputs are finite; a program needn't handle non-finite values.
Results may differ from the reference program's by a relative error of at most 0.025.
Values may be sent and summed in bfloat16 or wider, within the bound.
No kernel may reach another device: no remote copies, remote signals or barrier semaphores. Data moves between devices by JAX's collectives and lax.ppermute only.
A program may use at most 64 MiB of HBM per device.

```python
import math
import jax
import jax.numpy as jnp
from jax import lax

TILE = 2048
NRHS = 2
ITERS = 3
PAIR_DEV = 5
CITY_TILES = 32
TILES = 512
POINTS = 1048576


def city_orders(key):
    cities = TILES // CITY_TILES
    city_keys = jax.random.split(key, cities)
    return jax.vmap(lambda city_key: jax.random.permutation(city_key, CITY_TILES))(city_keys).astype(jnp.int32)


def point_layout(key):
    orders = city_orders(key)
    cities = TILES // CITY_TILES
    slot_of = jnp.argsort(orders, axis=1, stable=True).astype(jnp.int32)
    global_slot = (jnp.arange(cities, dtype=jnp.int32)[:, None] * CITY_TILES + slot_of).reshape(TILES)
    per_point = jnp.repeat(global_slot, TILE).astype(jnp.float32)
    key_x, key_y = jax.random.split(jax.random.fold_in(key, 5))
    across = jax.random.uniform(key_x, (TILES * TILE,), jnp.float32)
    along_y = jax.random.uniform(key_y, (TILES * TILE,), jnp.float32)
    return (per_point, across, along_y)


def draw_coords(key, part):
    per_point, across, along_y = point_layout(key)
    return jnp.stack([(per_point + across) * 1.25, along_y * 16.0]).astype(jnp.float32)


def draw_pair_list(key, part):
    orders = city_orders(key)
    key = jax.random.fold_in(key, 9)
    cities = TILES // CITY_TILES
    entry_count = 2 * CITY_TILES + 1
    entry_ids = jnp.arange(entry_count, dtype=jnp.int32)
    slot_ids = jnp.where(entry_ids < 5, 0, jnp.where(entry_ids < 9, 1, 2 + (entry_ids - 9) // 2))
    slot_place = jnp.where(entry_ids < 5, entry_ids, jnp.where(entry_ids < 9, entry_ids - 5, (entry_ids - 9) % 2))

    def one_city(city_id, city_key):
        own_order = orders[city_id]
        after_order = orders[(city_id + 1) % cities]
        before_order = orders[(city_id + cities - 1) % cities]
        tile_ids = jnp.arange(CITY_TILES, dtype=jnp.int32)
        self_pairs = jnp.stack([tile_ids, tile_ids, jnp.ones_like(tile_ids)], axis=1)
        chain_pairs = jnp.stack([own_order[:-1], own_order[1:], jnp.ones((CITY_TILES - 1,), jnp.int32)], axis=1)
        has_next = (city_id < cities - 1).astype(jnp.int32)
        has_prev = (city_id > 0).astype(jnp.int32)
        next_pair = jnp.stack([own_order[CITY_TILES - 1] * has_next, after_order[0] * has_next, 2 * has_next])[None, :]
        behind = jnp.stack([own_order[0] * has_prev, before_order[CITY_TILES - 1] * has_prev, 3 * has_prev])[None, :]
        entries = jnp.concatenate([self_pairs, chain_pairs, next_pair, behind], axis=0).astype(jnp.int32)
        key_order, key_owner = jax.random.split(city_key)
        entries = entries[jax.random.permutation(key_order, entry_count)]
        owner_ids = jax.random.permutation(key_owner, CITY_TILES)[slot_ids]
        slots_table = jnp.zeros((CITY_TILES, PAIR_DEV, 3), jnp.int32)
        return slots_table.at[owner_ids, slot_place].set(entries)
    tables = jax.vmap(one_city)(jnp.arange(cities, dtype=jnp.int32), jax.random.split(key, cities))
    return tables.reshape(TILES, PAIR_DEV, 3).astype(jnp.int32)


def draw_right_side(key, part):
    per_point, across, along_y = point_layout(key)
    key = jax.random.fold_in(key, 13)
    key_main = jax.random.fold_in(key, 0)
    key_scale = jax.random.fold_in(key, 1)
    key_phase = jax.random.fold_in(key, 3)
    east = (per_point + across) * 1.25
    north = along_y * 16.0
    phases = jax.random.uniform(key_phase, (2, NRHS), jnp.float32, 0.0, 6.2831853)
    wave = jnp.sin(east[None, :] * (6.2831853 / 7.0) + phases[0][:, None]) * jnp.cos(north[None, :] * (6.2831853 / 9.0) + phases[1][:, None])
    tile_pos = (jnp.arange(TILES * TILE) // TILE).astype(jnp.float32) / max(TILES - 1, 1)
    column_ids = jnp.arange(NRHS)
    rising = jnp.where((column_ids % 2 == 0)[:, None], jnp.power(3.0, -tile_pos)[None, :], jnp.power(3.0, tile_pos - 1.0)[None, :])
    column_scale = jnp.exp(jax.random.uniform(key_scale, (NRHS,), jnp.float32, jnp.log(0.5), jnp.log(5.0)))
    values = 0.7 * jnp.clip(jax.random.normal(key_main, (NRHS, TILES * TILE), jnp.float32), -4.5, 4.5)
    values = values + 1.5 * wave
    return (values * column_scale[:, None] * rising).astype(jnp.float32)


def with_ends(result, key, least, top_value):
    longest = result.shape.index(max(result.shape))
    spots = []
    for shift in (0, 1):
        where = [jax.random.randint(jax.random.fold_in(key, axis), (), 0, length) for axis, length in enumerate(result.shape)]
        where[longest] = (where[longest] + shift) % result.shape[longest]
        spots.append(tuple(where))
    return result.at[spots[0]].set(least).at[spots[1]].set(top_value)


def block_scale(rng, extent, shards, low, top_value):
    factor_of, own = 1.0, jax.random.fold_in(rng, 6)
    for position, parts in shards:
        heights = jnp.exp(jax.random.uniform(jax.random.fold_in(own, position), (parts,), jnp.float32, low / len(shards), top_value / len(shards)))
        factor_of = factor_of * jnp.repeat(heights, extent[position] // parts).reshape([-1 if axis == position else 1 for axis in range(len(extent))])
    return factor_of


def setup_inputs(seed: int = 0) -> dict:
    streams_of = jax.random.split(jax.random.key(seed), 6)
    right_side = draw_right_side(jax.random.fold_in(streams_of[5], 71), 0)
    noise_var = jnp.clip(jnp.exp(math.log(1.0) - 2.3025851 * jax.random.uniform(streams_of[1], (POINTS,), jnp.float32) ** block_scale(streams_of[1], (POINTS,), ((0, 512),), -0.2, 0.2)), 0.1, 1.0)
    coords = draw_coords(jax.random.fold_in(streams_of[5], 71), 0)
    counts = with_ends(jax.random.randint(streams_of[3], (TILES,), TILE // 2, TILE + 1), jax.random.fold_in(streams_of[3], 1), TILE // 2, TILE).astype(jnp.int32)
    pair_list = draw_pair_list(jax.random.fold_in(streams_of[5], 71), 0)
    return dict(right_side=right_side, noise_var=noise_var, coords=coords, counts=counts, pair_list=pair_list)


def wendland(near_pts, far_pts):
    across = near_pts[0][:, None] - far_pts[0][None, :]
    along_y = near_pts[1][:, None] - far_pts[1][None, :]
    reach = jnp.sqrt(across * across + along_y * along_y)
    inside = jnp.maximum(1.0 - reach, 0.0)
    square = inside * inside
    return square * square * (4.0 * reach + 1.0)

def to_bfloat(values):
    return lax.optimization_barrier(values.astype(jnp.bfloat16)).astype(jnp.float32)

def reference(right_side, noise_var, coords, counts, pair_list):
    valid_mask = (jnp.arange(TILE)[None, :] < counts[:, None]).astype(jnp.float32).reshape(TILES * TILE)
    noise_eff = jnp.where(valid_mask > 0, noise_var, 1.0).astype(jnp.float32)
    flat_pairs = pair_list.reshape(TILES * PAIR_DEV, 3)
    city_id = jnp.arange(TILES * PAIR_DEV) // PAIR_DEV // CITY_TILES
    pair_kind = flat_pairs[:, 2].astype(jnp.int32)
    city_shift = (pair_kind == 2).astype(jnp.int32) - (pair_kind == 3).astype(jnp.int32)
    near_tile = (city_id * CITY_TILES + flat_pairs[:, 0]).astype(jnp.int32)
    far_tile = jnp.clip(city_id * CITY_TILES + flat_pairs[:, 1] + CITY_TILES * city_shift, 0, TILES - 1).astype(jnp.int32)
    both_ways = ((pair_kind == 1) & (flat_pairs[:, 0] != flat_pairs[:, 1])).astype(jnp.int32)
    rows = (near_tile, far_tile, pair_kind, both_ways)

    def apply(direction):
        rounded_dirs = direction.astype(jnp.bfloat16)

        def add_pair(summed, row):
            near_id, far_id, kind_now, twice = row

            def compute(current):
                near_start = (near_id * TILE).astype(jnp.int32)
                far_start = (far_id * TILE).astype(jnp.int32)
                near_pts = lax.dynamic_slice_in_dim(coords, near_start, TILE, 1)
                far_pts = lax.dynamic_slice_in_dim(coords, far_start, TILE, 1)
                kernel = wendland(near_pts, far_pts).astype(jnp.bfloat16)
                near_vec = lax.dynamic_slice_in_dim(rounded_dirs, near_start, TILE, 1)
                far_vec = lax.dynamic_slice_in_dim(rounded_dirs, far_start, TILE, 1)
                to_near = lax.dot_general(far_vec, kernel, (((1,), (1,)), ((), ())), preferred_element_type=jnp.float32)
                to_far = jnp.dot(near_vec, kernel, preferred_element_type=jnp.float32)
                to_near = to_bfloat(to_near)
                to_far = to_bfloat(to_far) * twice.astype(jnp.float32)
                old_near = lax.dynamic_slice_in_dim(current, near_start, TILE, 1)
                current = lax.dynamic_update_slice_in_dim(current, old_near + to_near, near_start, 1)
                old_far = lax.dynamic_slice_in_dim(current, far_start, TILE, 1)
                return lax.dynamic_update_slice_in_dim(current, old_far + to_far, far_start, 1)
            return (lax.cond(kind_now > 0, compute, lambda unchanged: unchanged, summed), None)
        summed, _ = lax.scan(add_pair, jnp.zeros((NRHS, TILES * TILE), jnp.float32), rows)
        return valid_mask[None, :] * summed + noise_eff[None, :] * direction
    residual = right_side * valid_mask[None, :]
    direction = residual
    solution_field = jnp.zeros_like(residual)
    norm_now = lax.optimization_barrier(jnp.sum(residual * residual, axis=1))
    for iteration in range(ITERS):
        applied = apply(direction)
        curvature = lax.optimization_barrier(jnp.sum(direction * applied, axis=1))
        step_size = norm_now / curvature
        solution_field = solution_field + step_size[:, None] * direction
        residual = residual - step_size[:, None] * applied
        if iteration + 1 < ITERS:
            norm_next = lax.optimization_barrier(jnp.sum(residual * residual, axis=1))
            direction = residual + (norm_next / norm_now)[:, None] * direction
            norm_now = norm_next
    return (solution_field, residual)
```

```python
import jax
import jax.numpy as jnp
from jax import lax
from jax.experimental import pallas as pl
from jax.experimental.pallas import tpu as pltpu
from jax.sharding import PartitionSpec as P

SLOTS = 3
LANES = 128
SCALE = 4.0**0.2
HEAD = 5.0 / SCALE**4


def exchange_list(size, step):
    return [(i, i ^ step) for i in range(size)]


def tile_gather(block):
    size = lax.axis_size("tile")
    step = size // 2
    while step >= 1:
        other = lax.ppermute(block, "tile", exchange_list(size, step))
        block = jnp.concatenate([block, other], axis=0)
        step //= 2
    return block


def slot_of(tile):
    size = lax.axis_size("tile")
    bits = size.bit_length() - 1
    apart = jnp.bitwise_xor(tile, lax.axis_index("tile"))
    slot = jnp.zeros_like(apart)
    for bit in range(bits):
        slot = slot | (((apart >> bit) & 1) << (bits - 1 - bit))
    return slot


def axis_sum(values, axis):
    size = lax.axis_size(axis)
    step = 1
    while step < size:
        values = values + lax.ppermute(values, axis, exchange_list(size, step))
        step *= 2
    return values


def pick_tile(gathered, tile, length):
    picked = lax.dynamic_index_in_dim(gathered, slot_of(tile), 0, False)
    return picked[:, :length]


def city_moves():
    size = lax.axis_size("city")
    up = [(i, i + 1) for i in range(size - 1)]
    return up, [(j, i) for i, j in up]


def two_terms(values):
    high = values.astype(jnp.bfloat16).astype(jnp.float32)
    return jnp.concatenate([high, values - high], axis=0).astype(jnp.bfloat16)


def build_kernel(live, near_ref, far_ref, vec_ref, block_ref, out_ref):
    slot, part = pl.program_id(0), pl.program_id(1)
    rows, length = block_ref.shape[1:]
    width = min(1024, length)

    @pl.when((slot == 0) & (part == 0))
    def _():
        out_ref[...] = jnp.zeros_like(out_ref)

    @pl.when(live[slot] > 0)
    def _():
        far = jnp.transpose(far_ref[0])
        for top in range(0, rows, 16):
            far_x = far[top : top + 16, 0:1]
            far_y = far[top : top + 16, 1:2]
            for left in range(0, length, width):
                across = far_x - near_ref[0:1, left : left + width]
                along = far_y - near_ref[1:2, left : left + width]
                square = jnp.maximum(across * across + along * along, 1e-30)
                inside = jnp.maximum(SCALE - square * lax.rsqrt(square), 0.0)
                power = inside * inside
                value = power * power * (HEAD - inside)
                block_ref[0, top : top + 16, left : left + width] = value.astype(jnp.bfloat16)
        out_ref[...] += jnp.dot(
            two_terms(vec_ref[0]), block_ref[0], preferred_element_type=jnp.float32
        )


def apply_kernel(live, vec_ref, block_ref, out_ref):
    slot, part = pl.program_id(0), pl.program_id(1)

    @pl.when((slot == 0) & (part == 0))
    def _():
        out_ref[...] = jnp.zeros_like(out_ref)

    @pl.when(live[slot] > 0)
    def _():
        out_ref[...] += jnp.dot(
            two_terms(vec_ref[0]), block_ref[0], preferred_element_type=jnp.float32
        )


def eight_rows(values):
    return jnp.pad(values, ((0, 0), (0, 8 - values.shape[1]), (0, 0)))


def build(live, near, far, vecs):
    length = near.shape[1]
    rows = min(256, length)
    blocks, out = pl.pallas_call(
        build_kernel,
        grid_spec=pltpu.PrefetchScalarGridSpec(
            num_scalar_prefetch=1,
            grid=(SLOTS, length // rows),
            in_specs=[
                pl.BlockSpec((8, length), lambda s, p, live: (0, 0)),
                pl.BlockSpec((1, 8, rows), lambda s, p, live: (s, 0, p)),
                pl.BlockSpec((1, 8, rows), lambda s, p, live: (s, 0, p)),
            ],
            out_specs=[
                pl.BlockSpec((1, rows, length), lambda s, p, live: (s, p, 0)),
                pl.BlockSpec((16, length), lambda s, p, live: (0, 0)),
            ],
        ),
        out_shape=[
            jax.ShapeDtypeStruct((SLOTS, length, length), jnp.bfloat16),
            jax.ShapeDtypeStruct((16, length), jnp.float32),
        ],
        compiler_params=pltpu.CompilerParams(vmem_limit_bytes=32 * 1024 * 1024),
        cost_estimate=pl.CostEstimate(
            flops=SLOTS * length * length * 16,
            bytes_accessed=SLOTS * length * length * 2,
            transcendentals=SLOTS * length * length,
        ),
        name="build",
    )(live, jnp.pad(near, ((0, 6), (0, 0))), eight_rows(far), eight_rows(vecs))
    return blocks, out[0:2] + out[8:10]


def apply(live, vecs, blocks):
    length = vecs.shape[2]
    rows = min(256, length)
    out = pl.pallas_call(
        apply_kernel,
        grid_spec=pltpu.PrefetchScalarGridSpec(
            num_scalar_prefetch=1,
            grid=(SLOTS, length // rows),
            in_specs=[
                pl.BlockSpec((1, 8, rows), lambda s, p, live: (s, 0, p)),
                pl.BlockSpec((1, rows, length), lambda s, p, live: (s, p, 0)),
            ],
            out_specs=pl.BlockSpec((16, length), lambda s, p, live: (0, 0)),
        ),
        out_shape=jax.ShapeDtypeStruct((16, length), jnp.float32),
        compiler_params=pltpu.CompilerParams(vmem_limit_bytes=32 * 1024 * 1024),
        cost_estimate=pl.CostEstimate(
            flops=SLOTS * length * length * 16,
            bytes_accessed=SLOTS * length * length * 2,
            transcendentals=0,
        ),
        name="apply",
    )(live, eight_rows(vecs), blocks)
    return out[0:2] + out[8:10]


def dots(pairs):
    sums = [jnp.sum(a * b, axis=1) for a, b in pairs]
    return jnp.pad(jnp.stack(sums, axis=1), ((0, 0), (0, LANES - len(sums))))


def body(right_side, noise_var, coords, counts, pair_list):
    own = lax.axis_index("tile")
    size = lax.axis_size("tile")
    length = right_side.shape[1]
    up, down = city_moves()
    valid_mask = (jnp.arange(length) < counts[0]).astype(jnp.float32)
    noise_eff = jnp.where(valid_mask > 0, noise_var, 1.0)
    res_0 = right_side * valid_mask[None, :]

    table = pair_list.reshape(1, -1).astype(jnp.float32)
    entries = table.shape[1]
    table = jnp.pad(table, ((0, 1), (0, LANES - entries)))
    gathered = tile_gather(jnp.concatenate([res_0, table], axis=1)[None])
    rows = gathered[:, 0, length : length + entries].reshape(-1, 3).astype(jnp.int32)
    first, second, kind = rows[:, 0], rows[:, 1], rows[:, 2]

    shift = jnp.where(kind == 2, size, jnp.where(kind == 3, 2 * size, 0))
    code_near = jnp.where((kind > 0) & (first == own), second + shift, -1)
    code_far = jnp.where((kind == 1) & (first != second) & (second == own), first, -1)
    codes = jnp.concatenate([code_near, code_far])
    code = [jnp.max(codes)]
    for _ in range(SLOTS - 1):
        code.append(jnp.max(jnp.where(codes < code[-1], codes, -1)))
    live = jnp.stack([(c >= 0).astype(jnp.int32) for c in code])
    up_tile = jnp.maximum(jnp.max(jnp.where(kind == 2, first, -1)), 0)
    down_tile = jnp.maximum(jnp.max(jnp.where(kind == 3, first, -1)), 0)

    def coords_of(tile):
        return lax.dynamic_slice_in_dim(coords, tile * length, length, 1)

    def select(here, from_next, from_prev, number):
        return jnp.where(number < size, here, jnp.where(number < 2 * size, from_next, from_prev))

    def partners(gathered, extra_of=None):
        ups = pick_tile(gathered, up_tile, length)
        downs = pick_tile(gathered, down_tile, length)
        if extra_of is not None:
            ups = jnp.concatenate([ups, extra_of(up_tile)])
            downs = jnp.concatenate([downs, extra_of(down_tile)])
        from_prev = lax.ppermute(ups, "city", up)
        from_next = lax.ppermute(downs, "city", down)
        chosen = []
        for number in code:
            tile = jnp.bitwise_and(jnp.maximum(number, 0), size - 1)
            here = pick_tile(gathered, tile, length)
            if extra_of is not None:
                here = jnp.concatenate([here, extra_of(tile)])
            chosen.append(select(here, from_next, from_prev, number))
        return jnp.stack(chosen)

    def whole(summed, vec):
        return valid_mask[None, :] * summed + noise_eff[None, :] * vec

    chosen = partners(gathered, coords_of)
    near = coords_of(own)
    origin = near[:, 0:1]
    blocks, summed = build(
        live, (near - origin) * SCALE, (chosen[:, 2:4] - origin) * SCALE, chosen[:, 0:2]
    )
    img_0 = whole(summed, res_0)

    def exchange(vec, pairs):
        gathered = tile_gather(jnp.concatenate([vec, dots(pairs)], axis=1)[None])
        part = jnp.sum(gathered[:, :, length:], axis=0)
        totals = axis_sum(part, "city")[:, 0 : len(pairs)]
        return whole(apply(live, partners(gathered), blocks), vec), totals

    img_img_0, totals = exchange(img_0, [(res_0, res_0), (res_0, img_0), (img_0, img_0)])
    rr_0, curve_0, square_0 = totals[:, 0:1], totals[:, 1:2], totals[:, 2:3]
    step_1 = rr_0 / curve_0
    rr_1 = jnp.maximum(rr_0 - 2.0 * step_1 * curve_0 + step_1 * step_1 * square_0, 0.0)
    beta_1 = rr_1 / rr_0
    res_1 = res_0 - step_1 * img_0
    img_1 = img_0 - step_1 * img_img_0
    dir_1 = res_1 + beta_1 * res_0
    dir_img_1 = img_1 + beta_1 * img_0

    img_img_1, totals = exchange(
        img_1,
        [(res_1, res_1), (dir_1, dir_img_1), (res_1, dir_img_1), (dir_img_1, dir_img_1)],
    )
    rr_1, curve_1 = totals[:, 0:1], totals[:, 1:2]
    step_2 = rr_1 / curve_1
    rr_2 = rr_1 - 2.0 * step_2 * totals[:, 2:3] + step_2 * step_2 * totals[:, 3:4]
    beta_2 = jnp.maximum(rr_2, 0.0) / rr_1
    res_2 = res_1 - step_2 * dir_img_1
    img_2 = img_1 - step_2 * (img_img_1 + beta_1 * img_img_0)
    dir_2 = res_2 + beta_2 * dir_1
    dir_img_2 = img_2 + beta_2 * dir_img_1
    field_2 = step_1 * res_0 + step_2 * dir_1

    last = axis_sum(axis_sum(dots([(res_2, res_2), (dir_2, dir_img_2)]), "tile"), "city")
    step_3 = last[:, 0:1] / last[:, 1:2]
    return (field_2 + step_3 * dir_2, res_2 - step_3 * dir_img_2)


def solution(mesh):
    placed = (
        P(None, ("city", "tile")),
        P(("city", "tile")),
        P(None, "city"),
        P(("city", "tile")),
        P(("city", "tile"), None, None),
    )
    return jax.shard_map(
        body,
        mesh=mesh,
        in_specs=placed,
        out_specs=(P(None, ("city", "tile")), P(None, ("city", "tile"))),
        check_vma=False,
    )
```

```python
import functools

import jax
import jax.numpy as jnp
from jax import lax
from jax.experimental import pallas as pl
from jax.experimental.pallas import tpu as pltpu
from jax.sharding import PartitionSpec as P

ITERS = 3
LANES = 128
SCALE = 4.0**0.2
HEAD = 5.0 / SCALE**4
FAR = 1e18
PAIRS = [(i, j) for i in range(ITERS + 1) for j in range(i, ITERS + 1)]
SUM_ROWS = 24
OK_ROW = 2 * len(PAIRS)
GUARD = 3e-5
SMEM = pltpu.MemorySpace.SMEM
VMEM = pltpu.MemorySpace.VMEM


def padded(array, sides, width):
    for axis, dim in sides:
        size, length = (lax.axis_size(axis), array.shape[dim])
        up = [(i, (i + 1) % size) for i in range(size - 1)]
        down = [(j, i) for i, j in up]
        last = lax.slice_in_dim(array, length - width, length, axis=dim)
        leading = lax.slice_in_dim(array, 0, width, axis=dim)
        before = lax.ppermute(last, axis, up)
        after = lax.ppermute(leading, axis, down)
        array = jnp.concatenate([before, array, after], axis=dim)
    return array


def wendland(near_pts, far_pts):
    across = near_pts[0][:, None] - far_pts[0][None, :]
    along_y = near_pts[1][:, None] - far_pts[1][None, :]
    reach = jnp.sqrt(across * across + along_y * along_y)
    inside = jnp.maximum(1.0 - reach, 0.0)
    square = inside * inside
    return square * square * (4.0 * reach + 1.0)


def to_bfloat(values):
    return lax.optimization_barrier(values.astype(jnp.bfloat16)).astype(jnp.float32)


def any_graph(right_side, noise_var, coords, counts, pair_list):
    tile_count = lax.axis_size("tile")
    tile_len = right_side.shape[1]
    columns = right_side.shape[0]
    row_block = min(512, tile_len)
    valid_mask = (jnp.arange(tile_len) < counts[0]).astype(jnp.float32)
    noise_eff = jnp.where(valid_mask > 0, noise_var, 1.0)
    wide_coords = padded(coords, (("city", 1),), tile_count * tile_len)
    my_pairs = pair_list[0]
    slot_count = my_pairs.shape[0]

    def far_place(second_tile, pair_kind):
        city_shift = (pair_kind == 2).astype(jnp.int32) - (pair_kind == 3).astype(jnp.int32)
        return second_tile + tile_count * (1 + city_shift)

    def iterate(carry, _):
        residual, direction, solution_field, norm_now = carry
        own_dirs = direction.astype(jnp.bfloat16)
        city_dirs = lax.all_gather(own_dirs[None], "tile", axis=0, tiled=True)
        wide_dirs = padded(city_dirs, (("city", 0),), tile_count)

        def add_pair(slot_id, buffer):
            pair_row = lax.dynamic_index_in_dim(my_pairs, slot_id, 0, False)
            first_tile = pair_row[0]
            second_tile = pair_row[1]
            pair_kind = pair_row[2]
            far_tile = far_place(second_tile, pair_kind)

            def compute(current):
                near_pts = lax.dynamic_slice_in_dim(
                    wide_coords, (tile_count + first_tile) * tile_len, tile_len, 1
                )
                far_pts = lax.dynamic_slice_in_dim(wide_coords, far_tile * tile_len, tile_len, 1)
                near_vec = lax.dynamic_index_in_dim(city_dirs, first_tile, 0, False)
                far_vec = lax.dynamic_index_in_dim(wide_dirs, far_tile, 0, False)
                pieces = []
                back_sum = jnp.zeros((columns, tile_len), jnp.float32)
                for offset in range(0, tile_len, row_block):
                    kernel = wendland(near_pts[:, offset : offset + row_block], far_pts).astype(
                        jnp.bfloat16
                    )
                    pieces.append(
                        lax.dot_general(
                            far_vec,
                            kernel,
                            (((1,), (1,)), ((), ())),
                            preferred_element_type=jnp.float32,
                        )
                    )
                    back_sum = back_sum + jnp.dot(
                        near_vec[:, offset : offset + row_block],
                        kernel,
                        preferred_element_type=jnp.float32,
                    )
                to_near = to_bfloat(jnp.concatenate(pieces, axis=1))
                both_ways = ((pair_kind == 1) & (first_tile != second_tile)).astype(jnp.float32)
                to_far = to_bfloat(back_sum) * both_ways
                old_near = lax.dynamic_index_in_dim(current, first_tile, 0, False)
                current = lax.dynamic_update_index_in_dim(
                    current, old_near + to_near, first_tile, 0
                )
                old_far = lax.dynamic_index_in_dim(current, second_tile, 0, False)
                return lax.dynamic_update_index_in_dim(current, old_far + to_far, second_tile, 0)

            return lax.cond(pair_kind > 0, compute, lambda unchanged: unchanged, buffer)

        buffer = lax.fori_loop(
            0, slot_count, add_pair, jnp.zeros((tile_count, columns, tile_len), jnp.float32)
        )
        arrived = lax.all_to_all(
            buffer.astype(jnp.bfloat16), "tile", split_axis=0, concat_axis=0, tiled=True
        ).astype(buffer.dtype)
        summed = jnp.sum(arrived, axis=0)
        applied = valid_mask[None, :] * summed + noise_eff[None, :] * direction
        curvature = lax.psum(jnp.sum(direction * applied, axis=1), ("city", "tile"))
        step_size = norm_now / curvature
        solution_field = solution_field + step_size[:, None] * direction
        residual = residual - step_size[:, None] * applied
        norm_next = lax.psum(jnp.sum(residual * residual, axis=1), ("city", "tile"))
        direction = residual + (norm_next / norm_now)[:, None] * direction
        return (residual, direction, solution_field, norm_next), None

    residual = right_side * valid_mask[None, :]
    norm_now = lax.psum(jnp.sum(residual * residual, axis=1), ("city", "tile"))
    carry = (residual, residual, jnp.zeros_like(residual), norm_now)
    (residual, _, solution_field, _), _ = lax.scan(iterate, carry, None, length=ITERS)
    return (solution_field, residual)


def folded(ref, row):
    length = ref.shape[1]
    return jnp.concatenate(
        [ref[row : row + 1, left : left + LANES] for left in range(0, length, LANES)], axis=0
    )


def columns_of(rows):
    missing = LANES - rows.shape[0]
    return jnp.transpose(jnp.concatenate([rows, jnp.zeros((missing, LANES), rows.dtype)], axis=0))


def spread(rows, ref):
    turned = columns_of(rows)
    for c in range(rows.shape[0]):
        ref[c * LANES : (c + 1) * LANES, :] = jnp.broadcast_to(
            turned[:, c : c + 1], (LANES, LANES)
        )


def taken(values, source):
    chunk, lane = source // LANES, source % LANES
    result = jnp.zeros_like(values)
    for c in range(values.shape[0]):
        row = jnp.broadcast_to(values[c : c + 1, :], values.shape)
        result = jnp.where(chunk == c, jnp.take_along_axis(row, lane, axis=1), result)
    return result


def arrange_kernel(place, right_ref, noise_ref, coords_ref, table_ref, out_ref, rank_ref, wide):
    length = right_ref.shape[1]
    chunks = length // LANES
    lane = lax.broadcasted_iota(jnp.int32, (chunks, LANES), 1)
    index = lax.broadcasted_iota(jnp.int32, (chunks, LANES), 0) * LANES + lane
    valid = index < place[1]
    x, y = folded(coords_ref, 0), folded(coords_ref, 1)
    noise = jnp.where(valid, folded(noise_ref, 0), -1.0)
    right = [jnp.where(valid, folded(right_ref, r), 0.0) for r in range(2)]

    least = jnp.min(jnp.where(valid, y, FAR), keepdims=True)
    most = jnp.max(jnp.where(valid, y, -FAR), keepdims=True)
    bins = float(length - 1)
    level = jnp.floor((y - least) * (bins / jnp.maximum(most - least, 1e-6)))
    level = jnp.where(valid, jnp.clip(level, 0.0, bins), bins + 1.0)
    key = level * float(length) + index.astype(jnp.float32)

    def counted(rows, hit):
        def step(c, sums):
            column = wide[pl.ds(pl.multiple_of(c * LANES, LANES), LANES), :]
            found = []
            for r in range(chunks):
                terms = hit(column, rows[r : r + 1, :], c)
                found.append(sums[r] + jnp.sum(terms.reshape(LANES // 8, 8, LANES), axis=0))
            return tuple(found)

        zero = jnp.zeros((8, LANES), jnp.float32)
        sums = lax.fori_loop(0, chunks, step, (zero,) * chunks)
        return jnp.concatenate([jnp.sum(s, axis=0, keepdims=True) for s in sums], axis=0)

    spread(key, wide)
    rank = counted(key, lambda column, row, c: jnp.where(column < row, 1.0, 0.0))
    spread(rank, wide)
    within = lax.broadcasted_iota(jnp.int32, (LANES, LANES), 0)
    source = counted(
        index.astype(jnp.float32),
        lambda column, row, c: jnp.where(
            column == row, (within + c * LANES).astype(jnp.float32), 0.0
        ),
    ).astype(jnp.int32)
    rank_ref[...] = rank.astype(jnp.int32)
    for place_of, rows in enumerate((x, y, right[0], right[1], noise)):
        out_ref[place_of * chunks : (place_of + 1) * chunks, :] = taken(rows, source)
    out_ref[5 * chunks : 5 * chunks + 8, :] = table_ref[...]


def order_kernel(own, table, gathered, mine_ref, info, near_a, near_b, degree, order, sem):
    tiles = table.shape[0]

    def clear(t, _):
        degree[t] = 0
        near_a[t] = -1
        near_b[t] = -1
        return 0

    lax.fori_loop(0, tiles, clear, 0)

    def join(a, b):
        count = degree[a]

        @pl.when(count == 0)
        def _():
            near_a[a] = b

        @pl.when(count == 1)
        def _():
            near_b[a] = b

        degree[a] = count + 1

    for slot in range(8):
        info[slot] = 0
    info[5] = -1
    info[6] = -1

    def read(t, _):
        for slot in range(table.shape[1] // 3):
            kind = table[t, 3 * slot + 2]

            @pl.when(kind > 0)
            def _():
                a, b = table[t, 3 * slot], table[t, 3 * slot + 1]

                @pl.when(kind == 2)
                def _():
                    info[5] = a

                @pl.when(kind == 3)
                def _():
                    info[6] = a

                @pl.when((kind == 1) & (a == b))
                def _():
                    info[3] = info[3] + 1

                @pl.when((kind == 1) & (a != b))
                def _():
                    info[4] = info[4] + 1
                    join(a, b)
                    join(b, a)

        return 0

    lax.fori_loop(0, tiles, read, 0)
    selfs, edges, to_next, to_prev = info[3], info[4], info[5], info[6]

    def end_of(t, best):
        fits = (degree[t] <= 1) & (t != to_next) & (best < 0)
        return jnp.where(fits, t, best)

    start = lax.fori_loop(0, tiles, end_of, to_prev)
    complete = (start >= 0) & (selfs == tiles) & (edges == tiles - 1)

    def walk(p, carry):
        before, tile, good = carry
        order[p] = tile
        good = good & (degree[tile] <= 2)

        @pl.when(tile == own[0])
        def _():
            info[1] = p

        a, b = near_a[tile], near_b[tile]
        following = jnp.where(a != before, a, b)
        good = good & ((following >= 0) | (p == tiles - 1))
        return tile, jnp.maximum(following, 0), good

    first = jnp.maximum(start, 0)
    _, _, good = lax.fori_loop(0, tiles, walk, (jnp.int32(-1), first, complete))
    last = order[tiles - 1]
    good = good & ((to_prev < 0) | (degree[first] <= 1)) & (degree[last] <= 1)
    good = good & ((to_next < 0) | (last == to_next))
    tile = order[own[0]]
    info[0] = tile
    info[2] = good.astype(jnp.int32)
    info[3] = ((own[0] > 0) | (to_prev >= 0)).astype(jnp.int32)
    info[4] = ((own[0] < tiles - 1) | (to_next >= 0)).astype(jnp.int32)
    copy = pltpu.make_async_copy(gathered.at[tile], mine_ref, sem)
    copy.start()
    copy.wait()


def apply_kernel(
    base, info, mine, before, after, vec_0, vec_1, vec_2, out_ref, near_x, near_y, far, low, high
):
    chunks = out_ref.shape[0] // 2
    tiles, vecs = (mine, before, after), (vec_0, vec_1, vec_2)
    origin_x, origin_y = mine[0:1, 0:1], mine[chunks : chunks + 1, 0:1]

    def box(ref):
        good = ref[4 * chunks : 5 * chunks, :] >= 0.0
        sides = []
        for row in (0, chunks):
            values = ref[row : row + chunks, :]
            sides.append(jnp.min(jnp.where(good, values, FAR), axis=1, keepdims=True))
            sides.append(jnp.max(jnp.where(good, values, -FAR), axis=1, keepdims=True))
        return sides

    near_box = box(mine)
    for slot, ref in enumerate(tiles):
        far_box = near_box if slot == 0 else box(ref)
        least = jnp.full((chunks, 1), float(chunks), jnp.float32)
        most = jnp.zeros((chunks, 1), jnp.float32)
        for c in range(chunks):
            f = [side[c : c + 1, :] for side in far_box]
            gap_x = jnp.maximum(jnp.maximum(near_box[0] - f[1], f[0] - near_box[1]), 0.0)
            gap_y = jnp.maximum(jnp.maximum(near_box[2] - f[3], f[2] - near_box[3]), 0.0)
            close = gap_x * gap_x + gap_y * gap_y < 1.0001
            least = jnp.where(close, jnp.minimum(least, float(c // 2)), least)
            most = jnp.where(close, float(c // 2 + 1), most)
        for c in range(chunks):
            low[slot, c] = jnp.max(least[c : c + 1, :]).astype(jnp.int32)
            top = jnp.max(most[c : c + 1, :]).astype(jnp.int32)
            high[slot, c] = top if slot == 0 else top * info[2 + slot]
        far[slot, 0:chunks, :] = (ref[0:chunks, :] - origin_x) * SCALE
        far[slot, chunks : 2 * chunks, :] = (ref[chunks : 2 * chunks, :] - origin_y) * SCALE
    spread(far[0, 0:chunks, :], near_x)
    spread(far[0, chunks : 2 * chunks, :], near_y)
    groups = LANES // 8

    def near_chunk(i, _):
        sums = tuple(jnp.zeros((8, LANES), jnp.float32) for _ in range(2 * groups))
        for slot in range(3):

            def far_chunks(j, sums):
                found = list(sums)
                cells = []
                for h in range(2):
                    c = 2 * j + h
                    cells.append(
                        (
                            far[slot, pl.ds(c, 1), :],
                            far[slot, pl.ds(chunks + c, 1), :],
                            vecs[slot][pl.ds(base + c, 1), :],
                            vecs[slot][pl.ds(base + chunks + c, 1), :],
                        )
                    )
                for g in range(groups):
                    here = pl.ds(pl.multiple_of(i * LANES + 8 * g, 8), 8)
                    x, y = near_x[here, :], near_y[here, :]
                    for far_x, far_y, v_0, v_1 in cells:
                        across, along = x - far_x, y - far_y
                        square = jnp.maximum(across * across + along * along, 1e-30)
                        inside = jnp.maximum(SCALE - square * lax.rsqrt(square), 0.0)
                        power = inside * inside
                        value = power * power * (HEAD - inside)
                        found[2 * g] = found[2 * g] + value * v_0
                        found[2 * g + 1] = found[2 * g + 1] + value * v_1
                return tuple(found)

            sums = lax.fori_loop(low[slot, i], high[slot, i], far_chunks, sums)
        noise = mine[pl.ds(4 * chunks + i, 1), :]
        for r in range(2):
            block = jnp.concatenate(sums[r::2], axis=0)
            total = jnp.sum(jnp.transpose(block), axis=0, keepdims=True)
            own = vec_0[pl.ds(base + r * chunks + i, 1), :]
            out_ref[pl.ds(r * chunks + i, 1), :] = jnp.where(noise >= 0.0, total + noise * own, own)
        return 0

    lax.fori_loop(0, chunks, near_chunk, 0)


def sums_kernel(info, mine, vec_1, vec_2, vec_3, out_ref):
    chunks = vec_1.shape[0] // 2
    vecs = (mine[2 * chunks : 4 * chunks, :], vec_1[...], vec_2[...], vec_3[...])
    rows = []
    for r in range(2):
        half = [v[r * chunks : (r + 1) * chunks, :] for v in vecs]
        rows += [jnp.sum(half[i] * half[j], axis=0, keepdims=True) for i, j in PAIRS]
    rows.append(jnp.full((1, LANES), 1.0, jnp.float32) * info[2].astype(jnp.float32))
    rows.append(jnp.zeros((SUM_ROWS - len(rows), LANES), jnp.float32))
    out_ref[...] = jnp.concatenate(rows, axis=0)


def finish_kernel(devices, info, vecs_ref, sums_ref, home, rank, field_ref, residual_ref, ok_ref):
    chunks = rank.shape[0]
    total = jnp.sum(jnp.sum(sums_ref[...], axis=0), axis=1, keepdims=True)
    good = total[OK_ROW : OK_ROW + 1, :] == float(devices * LANES)
    places = rank[...]
    for r in range(2):
        gram = {}
        for k, (i, j) in enumerate(PAIRS):
            row = r * len(PAIRS) + k
            gram[i, j] = gram[j, i] = total[row : row + 1, :]

        def form(a, b):
            terms = [a[i] * b[j] * gram[i, j] for i in a for j in b]
            value, size = terms[0], jnp.abs(terms[0])
            for term in terms[1:]:
                value, size = value + term, size + jnp.abs(term)
            return value, value > GUARD * size

        def plus(a, scale, b):
            keys = sorted(set(a) | set(b))
            return {
                k: a[k] + scale * b[k] if k in a and k in b else (a[k] if k in a else scale * b[k])
                for k in keys
            }

        one = jnp.ones((1, 1), jnp.float32)
        res, direction, field = {0: one}, {0: one}, {}
        norm, fine = form(res, res)
        good = good & fine
        for iteration in range(ITERS):
            image = {k + 1: v for k, v in direction.items()}
            curve, fine = form(direction, image)
            good = good & fine
            step = norm / curve
            field = plus(field, step, direction)
            res = plus(res, -step, image)
            if iteration + 1 < ITERS:
                new, fine = form(res, res)
                good = good & fine
                direction = plus(res, new / norm, direction)
                norm = new

        def vec(k):
            if k == 0:
                return home[(2 + r) * chunks : (3 + r) * chunks, :]
            row = (2 * (k - 1) + r) * chunks
            return vecs_ref[0, row : row + chunks, :]

        for ref, weights in ((field_ref, field), (residual_ref, res)):
            values = taken(sum(w * vec(k) for k, w in weights.items()), places)
            for c in range(chunks):
                ref[r : r + 1, c * LANES : (c + 1) * LANES] = values[c : c + 1, :]
    ok_ref[...] = jnp.where(good, 1.0, 0.0) * jnp.ones((8, LANES), jnp.float32)


def whole(shape):
    return pl.BlockSpec(shape, lambda i, *_: (0,) * len(shape))


def params(mib=16):
    return pltpu.CompilerParams(vmem_limit_bytes=mib * 1024 * 1024)


def body(right_side, noise_var, coords, counts, pair_list):
    own = lax.axis_index("tile").astype(jnp.int32)
    tiles, cities = lax.axis_size("tile"), lax.axis_size("city")
    length = right_side.shape[1]
    chunks = length // LANES
    rows = 5 * chunks + 8
    table = pair_list.reshape(1, -1).astype(jnp.float32)
    entries = table.shape[1]
    table = jnp.pad(table, ((0, 7), (0, LANES - entries)))
    f32 = functools.partial(jax.ShapeDtypeStruct, dtype=jnp.float32)

    home, rank = pl.pallas_call(
        arrange_kernel,
        grid_spec=pltpu.PrefetchScalarGridSpec(
            num_scalar_prefetch=1,
            grid=(1,),
            in_specs=[
                whole((2, length)),
                whole((1, length)),
                pl.BlockSpec((2, length), lambda i, place: (0, place[0])),
                whole((8, LANES)),
            ],
            out_specs=[whole((rows, LANES)), whole((chunks, LANES))],
            scratch_shapes=[pltpu.VMEM((length, LANES), jnp.float32)],
        ),
        out_shape=[f32((rows, LANES)), jax.ShapeDtypeStruct((chunks, LANES), jnp.int32)],
        compiler_params=params(),
        name="arrange",
    )(jnp.stack([own, counts[0]]), right_side, noise_var[None, :], coords, table)

    gathered = lax.all_gather(home, "tile")
    city_table = gathered[:, 5 * chunks, :entries].astype(jnp.int32)
    mine, info = pl.pallas_call(
        order_kernel,
        in_specs=[
            pl.BlockSpec(memory_space=SMEM),
            pl.BlockSpec(memory_space=SMEM),
            pl.BlockSpec(memory_space=pl.ANY),
        ],
        out_specs=[pl.BlockSpec(memory_space=VMEM), pl.BlockSpec(memory_space=SMEM)],
        out_shape=[f32((rows, LANES)), jax.ShapeDtypeStruct((8,), jnp.int32)],
        scratch_shapes=[pltpu.SMEM((tiles,), jnp.int32)] * 4 + [pltpu.SemaphoreType.DMA],
        compiler_params=params(),
        name="order",
    )(own[None], city_table, gathered)

    forward = [(i, i + 1) for i in range(tiles * cities - 1)]
    backward = [(j, i) for i, j in forward]

    def neighbours(block):
        axes = ("city", "tile")
        return lax.ppermute(block, axes, forward), lax.ppermute(block, axes, backward)

    def apply(ends, vecs, base):
        size = vecs[0].shape[0]
        return pl.pallas_call(
            functools.partial(apply_kernel, base),
            grid_spec=pltpu.PrefetchScalarGridSpec(
                num_scalar_prefetch=1,
                grid=(1,),
                in_specs=[whole((rows, LANES))] * 3 + [whole((size, LANES))] * 3,
                out_specs=whole((2 * chunks, LANES)),
                scratch_shapes=[
                    pltpu.VMEM((length, LANES), jnp.float32),
                    pltpu.VMEM((length, LANES), jnp.float32),
                    pltpu.VMEM((3, 2 * chunks, LANES), jnp.float32),
                    pltpu.SMEM((3, chunks), jnp.int32),
                    pltpu.SMEM((3, chunks), jnp.int32),
                ],
            ),
            out_shape=f32((2 * chunks, LANES)),
            compiler_params=params(),
            name="apply",
        )(info, mine, *ends, *vecs)

    ends = neighbours(mine)
    vec_1 = apply(ends, (mine, *ends), 2 * chunks)
    vec_2 = apply(ends, (vec_1, *neighbours(vec_1)), 0)
    vec_3 = apply(ends, (vec_2, *neighbours(vec_2)), 0)

    sums = pl.pallas_call(
        sums_kernel,
        grid_spec=pltpu.PrefetchScalarGridSpec(
            num_scalar_prefetch=1,
            grid=(1,),
            in_specs=[whole((rows, LANES))] + [whole((2 * chunks, LANES))] * 3,
            out_specs=whole((SUM_ROWS, LANES)),
        ),
        out_shape=f32((SUM_ROWS, LANES)),
        compiler_params=params(),
        name="sums",
    )(info, mine, vec_1, vec_2, vec_3)
    sums = jnp.sum(lax.all_gather(sums, "city"), axis=0)
    back = lax.all_gather(jnp.concatenate([vec_1, vec_2, vec_3, sums], axis=0), "tile")
    size = 6 * chunks
    field, residual, good = pl.pallas_call(
        functools.partial(finish_kernel, tiles * cities),
        grid_spec=pltpu.PrefetchScalarGridSpec(
            num_scalar_prefetch=1,
            grid=(1,),
            in_specs=[
                pl.BlockSpec((1, size, LANES), lambda i, info: (info[1], 0, 0)),
                pl.BlockSpec((tiles, SUM_ROWS, LANES), lambda i, info: (0, size // SUM_ROWS, 0)),
                whole((rows, LANES)),
                whole((chunks, LANES)),
            ],
            out_specs=[whole((2, length)), whole((2, length)), whole((8, LANES))],
        ),
        out_shape=[f32((2, length)), f32((2, length)), f32((8, LANES))],
        compiler_params=params(),
        name="finish",
    )(info, back, back, home, rank)
    return lax.cond(
        good[0, 0] > 0.0,
        lambda *args: (field, residual),
        any_graph,
        right_side,
        noise_var,
        coords,
        counts,
        pair_list,
    )


def solution(mesh):
    placed = (
        P(None, ("city", "tile")),
        P(("city", "tile")),
        P(None, "city"),
        P(("city", "tile")),
        P(("city", "tile"), None, None),
    )
    return jax.shard_map(
        body,
        mesh=mesh,
        in_specs=placed,
        out_specs=(P(None, ("city", "tile")), P(None, ("city", "tile"))),
        check_vma=False,
    )
```

```python
import functools

import jax
import jax.numpy as jnp
from jax import lax
from jax.experimental import pallas as pl
from jax.experimental.pallas import tpu as pltpu
from jax.sharding import PartitionSpec as P

ITERS = 3
LANES = 128
SCALE = 4.0**0.2
HEAD = 5.0 / SCALE**4
FAR = 1e18
PAIRS = [(i, j) for i in range(ITERS + 1) for j in range(i, ITERS + 1)]
OK_ROW = 2 * len(PAIRS)
MADE = OK_ROW + 1
SUM_ROWS = 16
GUARD = 3e-5
KEPT = 136
MOST = 3.0
SMEM = pltpu.MemorySpace.SMEM
VMEM = pltpu.MemorySpace.VMEM
TILE = ("far", "near")


def padded(array, sides, width):
    for axis, dim in sides:
        size, length = (lax.axis_size(axis), array.shape[dim])
        up = [(i, (i + 1) % size) for i in range(size - 1)]
        down = [(j, i) for i, j in up]
        last = lax.slice_in_dim(array, length - width, length, axis=dim)
        leading = lax.slice_in_dim(array, 0, width, axis=dim)
        before = lax.ppermute(last, axis, up)
        after = lax.ppermute(leading, axis, down)
        array = jnp.concatenate([before, array, after], axis=dim)
    return array


def wendland(near_pts, far_pts):
    across = near_pts[0][:, None] - far_pts[0][None, :]
    along_y = near_pts[1][:, None] - far_pts[1][None, :]
    reach = jnp.sqrt(across * across + along_y * along_y)
    inside = jnp.maximum(1.0 - reach, 0.0)
    square = inside * inside
    return square * square * (4.0 * reach + 1.0)


def to_bfloat(values):
    return lax.optimization_barrier(values.astype(jnp.bfloat16)).astype(jnp.float32)


def any_graph(right_side, noise_var, coords, counts, pair_list):
    tile_count = lax.axis_size(TILE)
    tile_len = right_side.shape[1]
    columns = right_side.shape[0]
    row_block = min(512, tile_len)
    valid_mask = (jnp.arange(tile_len) < counts[0]).astype(jnp.float32)
    noise_eff = jnp.where(valid_mask > 0, noise_var, 1.0)
    wide_coords = padded(coords, (("city", 1),), tile_count * tile_len)
    my_pairs = pair_list[0]
    slot_count = my_pairs.shape[0]

    def far_place(second_tile, pair_kind):
        city_shift = (pair_kind == 2).astype(jnp.int32) - (pair_kind == 3).astype(jnp.int32)
        return second_tile + tile_count * (1 + city_shift)

    def iterate(carry, _):
        residual, direction, solution_field, norm_now = carry
        own_dirs = direction.astype(jnp.bfloat16)
        city_dirs = lax.all_gather(own_dirs[None], TILE, axis=0, tiled=True)
        wide_dirs = padded(city_dirs, (("city", 0),), tile_count)

        def add_pair(slot_id, buffer):
            pair_row = lax.dynamic_index_in_dim(my_pairs, slot_id, 0, False)
            first_tile = pair_row[0]
            second_tile = pair_row[1]
            pair_kind = pair_row[2]
            far_tile = far_place(second_tile, pair_kind)

            def compute(current):
                near_pts = lax.dynamic_slice_in_dim(
                    wide_coords, (tile_count + first_tile) * tile_len, tile_len, 1
                )
                far_pts = lax.dynamic_slice_in_dim(wide_coords, far_tile * tile_len, tile_len, 1)
                near_vec = lax.dynamic_index_in_dim(city_dirs, first_tile, 0, False)
                far_vec = lax.dynamic_index_in_dim(wide_dirs, far_tile, 0, False)
                pieces = []
                back_sum = jnp.zeros((columns, tile_len), jnp.float32)
                for offset in range(0, tile_len, row_block):
                    kernel = wendland(near_pts[:, offset : offset + row_block], far_pts).astype(
                        jnp.bfloat16
                    )
                    pieces.append(
                        lax.dot_general(
                            far_vec,
                            kernel,
                            (((1,), (1,)), ((), ())),
                            preferred_element_type=jnp.float32,
                        )
                    )
                    back_sum = back_sum + jnp.dot(
                        near_vec[:, offset : offset + row_block],
                        kernel,
                        preferred_element_type=jnp.float32,
                    )
                to_near = to_bfloat(jnp.concatenate(pieces, axis=1))
                both_ways = ((pair_kind == 1) & (first_tile != second_tile)).astype(jnp.float32)
                to_far = to_bfloat(back_sum) * both_ways
                old_near = lax.dynamic_index_in_dim(current, first_tile, 0, False)
                current = lax.dynamic_update_index_in_dim(
                    current, old_near + to_near, first_tile, 0
                )
                old_far = lax.dynamic_index_in_dim(current, second_tile, 0, False)
                return lax.dynamic_update_index_in_dim(current, old_far + to_far, second_tile, 0)

            return lax.cond(pair_kind > 0, compute, lambda unchanged: unchanged, buffer)

        buffer = lax.fori_loop(
            0, slot_count, add_pair, jnp.zeros((tile_count, columns, tile_len), jnp.float32)
        )
        arrived = lax.all_to_all(
            buffer.astype(jnp.bfloat16), TILE, split_axis=0, concat_axis=0, tiled=True
        ).astype(buffer.dtype)
        summed = jnp.sum(arrived, axis=0)
        applied = valid_mask[None, :] * summed + noise_eff[None, :] * direction
        curvature = lax.psum(jnp.sum(direction * applied, axis=1), ("city", *TILE))
        step_size = norm_now / curvature
        solution_field = solution_field + step_size[:, None] * direction
        residual = residual - step_size[:, None] * applied
        norm_next = lax.psum(jnp.sum(residual * residual, axis=1), ("city", *TILE))
        direction = residual + (norm_next / norm_now)[:, None] * direction
        return (residual, direction, solution_field, norm_next), None

    residual = right_side * valid_mask[None, :]
    norm_now = lax.psum(jnp.sum(residual * residual, axis=1), ("city", *TILE))
    carry = (residual, residual, jnp.zeros_like(residual), norm_now)
    (residual, _, solution_field, _), _ = lax.scan(iterate, carry, None, length=ITERS)
    return (solution_field, residual)


def folded(ref, row):
    length = ref.shape[1]
    return jnp.concatenate(
        [ref[row : row + 1, left : left + LANES] for left in range(0, length, LANES)], axis=0
    )


def columns_of(rows):
    missing = LANES - rows.shape[0]
    return jnp.transpose(jnp.concatenate([rows, jnp.zeros((missing, LANES), rows.dtype)], axis=0))


def spread(rows, ref):
    turned = columns_of(rows)
    for c in range(rows.shape[0]):
        ref[c * LANES : (c + 1) * LANES, :] = jnp.broadcast_to(
            turned[:, c : c + 1], (LANES, LANES)
        )


def taken(values, source):
    chunk, lane = source // LANES, source % LANES
    result = jnp.zeros_like(values)
    for c in range(values.shape[0]):
        row = jnp.broadcast_to(values[c : c + 1, :], values.shape)
        result = jnp.where(chunk == c, jnp.take_along_axis(row, lane, axis=1), result)
    return result


def pack_kernel(place, table, right_ref, noise_ref, out_ref):
    chunks = right_ref.shape[1] // LANES
    lane = lax.broadcasted_iota(jnp.int32, (chunks, LANES), 1)
    valid = lax.broadcasted_iota(jnp.int32, (chunks, LANES), 0) * LANES + lane < place[0]
    rows = [jnp.where(valid, folded(right_ref, r), 0.0) for r in range(2)]
    rows.append(jnp.where(valid, folded(noise_ref, 0), -1.0))
    entries = jnp.zeros((chunks, LANES), jnp.int32)
    for k in range(table.shape[0]):
        entries = jnp.where(lane == k, table[k], entries)
    rows.append(entries.astype(jnp.float32))
    out_ref[...] = jnp.concatenate(rows, axis=0).astype(jnp.bfloat16)


def arrange(mine, coords_ref, out_ref, rank_ref):
    length = coords_ref.shape[1]
    chunks = length // LANES
    lane = lax.broadcasted_iota(jnp.int32, (chunks, LANES), 1)
    index = lax.broadcasted_iota(jnp.int32, (chunks, LANES), 0) * LANES + lane
    x, y = folded(coords_ref, 0), folded(coords_ref, 1)
    packed = mine[...].astype(jnp.float32)
    right = [packed[r * chunks : (r + 1) * chunks, :] for r in range(2)]
    noise = packed[2 * chunks : 3 * chunks, :]
    valid = noise >= 0.0

    least = jnp.min(jnp.where(valid, y, FAR), keepdims=True)
    most = jnp.max(jnp.where(valid, y, -FAR), keepdims=True)
    top = float(LANES - 2)
    level = jnp.floor((y - least) * (top / jnp.maximum(most - least, 1e-6)))
    level = jnp.where(valid, jnp.clip(level, 0.0, top), top + 1.0)
    down = lax.broadcasted_iota(jnp.int32, (LANES, LANES), 0)
    along = lax.broadcasted_iota(jnp.int32, (LANES, LANES), 1)

    def dot(a, b, dims=((1,), (0,))):
        return lax.dot_general(
            a.astype(jnp.bfloat16),
            b.astype(jnp.bfloat16),
            (dims, ((), ())),
            preferred_element_type=jnp.float32,
        )

    def one_hot(rows, c):
        return jnp.where(down.astype(jnp.float32) == rows[c : c + 1, :], 1.0, 0.0)

    ones = jnp.ones((LANES, LANES), jnp.float32)
    counter = jnp.concatenate([jnp.where(down < along, 1.0, 0.0), ones], axis=1)
    running = jnp.zeros((LANES, LANES), jnp.float32)
    ahead = []
    for c in range(chunks):
        counted = dot(one_hot(level, c), counter)
        ahead.append(counted[:, 0:LANES] + running)
        running = running + counted[:, LANES:]
    tens = jnp.floor(running * (1.0 / 64.0))
    below = jnp.where(along < down, 1.0, 0.0)
    base = 64.0 * dot(below, tens) + dot(below, running - 64.0 * tens)
    rank = jnp.concatenate(
        [
            jnp.sum(one_hot(level, c) * (ahead[c] + base), axis=0, keepdims=True)
            for c in range(chunks)
        ],
        axis=0,
    ).astype(jnp.int32)
    rank_ref[...] = rank
    row_of, lane_of = rank // LANES, (rank % LANES).astype(jnp.float32)
    first = lax.broadcasted_iota(jnp.int32, (chunks, LANES), 0)
    lanes = lane.astype(jnp.float32)
    found = jnp.zeros((2 * chunks, LANES), jnp.float32)
    for c in range(chunks):
        there = first == row_of[c : c + 1, :]
        values = jnp.concatenate(
            [jnp.where(there, lanes, 0.0), jnp.where(there, float(c), 0.0)], axis=0
        )
        found = found + dot(values, one_hot(lane_of, c), ((1,), (1,)))
    source = (found[0:chunks, :] + LANES * found[chunks:, :]).astype(jnp.int32)
    for place_of, rows in enumerate((x, y, right[0], right[1], noise)):
        out_ref[place_of * chunks : (place_of + 1) * chunks, :] = taken(rows, source)


def order_kernel(
    own, table, gathered, coords, out_ref, rank_ref, info, links, degree, order, mine, points, sems
):
    tiles = table.shape[0]
    near = gathered.shape[0]
    length = points.shape[1]
    for t in range(tiles):
        degree[t] = 0
        links[2 * t] = -1
        links[2 * t + 1] = -1
    info[1] = 0

    def join(a, b):
        count = degree[a]
        links[2 * a + jnp.minimum(count, 1)] = b
        degree[a] = count + 1

    def read(t, carry):
        selfs, edges, to_next, to_prev = carry
        for slot in range(table.shape[1] // 3):
            a, b, kind = table[t, 3 * slot], table[t, 3 * slot + 1], table[t, 3 * slot + 2]
            pair = (kind == 1) & (a != b)
            selfs = selfs + ((kind == 1) & (a == b)).astype(jnp.int32)
            edges = edges + pair.astype(jnp.int32)
            to_next = jnp.where(kind == 2, a, to_next)
            to_prev = jnp.where(kind == 3, a, to_prev)

            @pl.when(pair)
            def _():
                join(a, b)
                join(b, a)

        return selfs, edges, to_next, to_prev

    zero, none = jnp.int32(0), jnp.int32(-1)
    found = lax.fori_loop(0, tiles, read, (zero, zero, none, none))
    selfs, edges, to_next, to_prev = found

    def end_of(t, best):
        fits = (degree[t] <= 1) & (t != to_next) & (best < 0)
        return jnp.where(fits, t, best)

    start = lax.fori_loop(0, tiles, end_of, to_prev)
    complete = (start >= 0) & (selfs == tiles) & (edges == tiles - 1)

    def walk(p, carry):
        before, tile, good = carry
        order[p] = tile
        good = good & (degree[tile] <= 2)

        @pl.when(tile == own[0])
        def _():
            info[1] = p

        a, b = links[2 * tile], links[2 * tile + 1]
        following = jnp.where(a != before, a, b)
        good = good & ((following >= 0) | (p == tiles - 1))
        return tile, jnp.maximum(following, 0), good

    first = jnp.maximum(start, 0)
    _, _, good = lax.fori_loop(0, tiles, walk, (jnp.int32(-1), first, complete))
    last = order[tiles - 1]
    good = good & ((to_prev < 0) | (degree[first] <= 1)) & (degree[last] <= 1)
    good = good & ((to_next < 0) | (last == to_next))
    tile = order[own[0]]
    info[0] = tile
    info[2] = good.astype(jnp.int32)
    info[3] = ((own[0] > 0) | (to_prev >= 0)).astype(jnp.int32)
    info[4] = ((own[0] < tiles - 1) | (to_next >= 0)).astype(jnp.int32)
    start_of = pl.multiple_of(tile * length, length)
    copies = [
        pltpu.make_async_copy(gathered.at[tile % near, tile // near], mine, sems.at[0]),
        pltpu.make_async_copy(coords.at[:, pl.ds(start_of, length)], points, sems.at[1]),
    ]
    for copy in copies:
        copy.start()
    for copy in copies:
        copy.wait()
    arrange(mine, points, out_ref, rank_ref)


def close_chunks(mine, before, after, info, bounds, far):
    chunks = far.shape[1] // 2
    origin_x, origin_y = mine[0:1, 0:1], mine[chunks : chunks + 1, 0:1]

    def box(ref):
        good = ref[4 * chunks : 5 * chunks, :] >= 0.0
        sides = []
        for row in (0, chunks):
            values = ref[row : row + chunks, :]
            sides.append(jnp.min(jnp.where(good, values, FAR), axis=1, keepdims=True))
            sides.append(jnp.max(jnp.where(good, values, -FAR), axis=1, keepdims=True))
        return sides

    near_box = box(mine)
    for slot, ref in enumerate((mine, before, after)):
        far_box = near_box if slot == 0 else box(ref)
        least = jnp.full((chunks, 1), float(chunks), jnp.float32)
        most = jnp.zeros((chunks, 1), jnp.float32)
        for c in range(chunks):
            f = [side[c : c + 1, :] for side in far_box]
            gap_x = jnp.maximum(jnp.maximum(near_box[0] - f[1], f[0] - near_box[1]), 0.0)
            gap_y = jnp.maximum(jnp.maximum(near_box[2] - f[3], f[2] - near_box[3]), 0.0)
            close = gap_x * gap_x + gap_y * gap_y < 1.0001
            least = jnp.where(close, jnp.minimum(least, float(c)), least)
            most = jnp.where(close, float(c + 1), most)
        pairs = jnp.floor(jnp.maximum(most - least + 1.0, 0.0) * 0.5)
        least = jnp.minimum(least, chunks - 2.0 * pairs)
        for c in range(chunks):
            bounds[slot * chunks + c] = jnp.max(least[c : c + 1, :]).astype(jnp.int32)
            count = jnp.max(pairs[c : c + 1, :]).astype(jnp.int32)
            bounds[(3 + slot) * chunks + c] = count if slot == 0 else count * info[2 + slot]
        far[slot, 0:chunks, :] = (ref[0:chunks, :] - origin_x) * SCALE
        far[slot, chunks : 2 * chunks, :] = (ref[chunks : 2 * chunks, :] - origin_y) * SCALE


def row_sums(bounds, base, mine, vecs, out_ref, block_of):
    chunks = out_ref.shape[0] // 2
    groups = LANES // 16

    def near_chunk(i, number):
        sums = tuple(jnp.zeros((16, LANES), jnp.float32) for _ in range(2 * groups))
        carry = (number, sums)
        for slot in range(3):

            def far_chunks(j, carry):
                number, sums = carry
                found = list(sums)
                rows = []
                start = bounds[slot * chunks + i] + 2 * j
                for h in range(2):
                    c = base + start + h
                    rows.append([vecs[slot][pl.ds(c + r * chunks, 1), :] for r in range(2)])
                for g, h, value in block_of(number, slot, i, start):
                    for r in range(2):
                        found[2 * g + r] = found[2 * g + r] + value * rows[h][r]
                return number + 1, tuple(found)

            carry = lax.fori_loop(0, bounds[(3 + slot) * chunks + i], far_chunks, carry)
        number, sums = carry
        noise = mine[pl.ds(4 * chunks + i, 1), :]
        for r in range(2):
            block = jnp.concatenate(sums[r::2], axis=0)
            total = jnp.sum(jnp.transpose(block), axis=0, keepdims=True)
            own = vecs[0][pl.ds(base + r * chunks + i, 1), :]
            out_ref[pl.ds(r * chunks + i, 1), :] = jnp.where(noise >= 0.0, total + noise * own, own)
        return number

    return lax.fori_loop(0, chunks, near_chunk, jnp.int32(0))


def evaluated(near_x, near_y, far, slot, i, start):
    chunks = far.shape[1] // 2
    cells = []
    for h in range(2):
        c = start + h
        cells.append((far[slot, pl.ds(c, 1), :], far[slot, pl.ds(chunks + c, 1), :]))
    for g in range(LANES // 16):
        here = pl.ds(pl.multiple_of(i * LANES + 16 * g, 16), 16)
        x, y = near_x[here, :], near_y[here, :]
        for h, (far_x, far_y) in enumerate(cells):
            across, along = x - far_x, y - far_y
            square = jnp.maximum(across * across + along * along, 1e-30)
            inside = jnp.maximum(SCALE - square * lax.rsqrt(square), 0.0)
            power = inside * inside
            yield g, h, power * power * (HEAD - inside)


def build_kernel(info, mine, before, after, out_ref, blocks, bounds, far, near_x, near_y):
    chunks = out_ref.shape[0] // 2
    close_chunks(mine, before, after, info, bounds, far)
    spread(far[0, 0:chunks, :], near_x)
    spread(far[0, chunks : 2 * chunks, :], near_y)

    def block_of(number, slot, i, start):
        place = jnp.minimum(number, blocks.shape[0] - 1)
        for g, h, value in evaluated(near_x, near_y, far, slot, i, start):
            blocks[place, 16 * g : 16 * g + 16, h * LANES : (h + 1) * LANES] = value.astype(
                jnp.bfloat16
            )
            yield g, h, value

    bounds[6 * chunks] = row_sums(
        bounds, 2 * chunks, mine, (mine, before, after), out_ref, block_of
    )


def apply_kernel(bounds, mine, vec_0, vec_1, vec_2, far, blocks, out_ref, near_x, near_y):
    chunks = out_ref.shape[0] // 2
    vecs = (vec_0, vec_1, vec_2)
    kept = bounds[6 * chunks] <= blocks.shape[0]

    @pl.when(kept)
    def _():
        def block_of(number, slot, i, start):
            for g in range(LANES // 16):
                for h in range(2):
                    value = blocks[number, 16 * g : 16 * g + 16, h * LANES : (h + 1) * LANES]
                    yield g, h, value.astype(jnp.float32)

        row_sums(bounds, 0, mine, vecs, out_ref, block_of)

    @pl.when(jnp.logical_not(kept))
    def _():
        spread(far[0, 0:chunks, :], near_x)
        spread(far[0, chunks : 2 * chunks, :], near_y)

        def block_of(number, slot, i, start):
            yield from evaluated(near_x, near_y, far, slot, i, start)

        row_sums(bounds, 0, mine, vecs, out_ref, block_of)


def sums_kernel(info, mine, vec_1, vec_2, vec_3, out_ref):
    chunks = vec_1.shape[0] // 2
    vecs = (mine[2 * chunks : 4 * chunks, :], vec_1[...], vec_2[...], vec_3[...])
    rows = []
    for r in range(2):
        half = [v[r * chunks : (r + 1) * chunks, :] for v in vecs]
        rows += [jnp.sum(half[i] * half[j], axis=0, keepdims=True) for i, j in PAIRS]
    rows.append(jnp.full((1, LANES), 1.0 / LANES, jnp.float32) * info[2].astype(jnp.float32))
    rows.append(jnp.zeros((LANES - len(rows), LANES), jnp.float32))
    turned = jnp.transpose(jnp.concatenate(rows, axis=0))
    out_ref[...] = jnp.broadcast_to(jnp.sum(turned, axis=0, keepdims=True), out_ref.shape)


def iterated(gram):
    def form(a, b):
        terms = [a[i] * b[j] * gram[i, j] for i in a for j in b]
        value, size = terms[0], jnp.abs(terms[0])
        for term in terms[1:]:
            value, size = value + term, size + jnp.abs(term)
        return value, value > GUARD * size

    def plus(a, scale, b):
        keys = sorted(set(a) | set(b))
        return {
            k: a[k] + scale * b[k] if k in a and k in b else (a[k] if k in a else scale * b[k])
            for k in keys
        }

    one = jnp.ones((1, 1), jnp.float32)
    res, direction, field = {0: one}, {0: one}, {}
    norm, good = form(res, res)
    residuals = []
    for iteration in range(ITERS):
        image = {k + 1: v for k, v in direction.items()}
        curve, fine = form(direction, image)
        good = good & fine
        step = norm / curve
        field = plus(field, step, direction)
        res = plus(res, -step, image)
        residuals.append(res)
        if iteration + 1 < ITERS:
            new, fine = form(res, res)
            good = good & fine
            direction = plus(res, new / norm, direction)
            norm = new
    return field, residuals, good


def gram_of(row, r):
    column = jnp.transpose(jnp.broadcast_to(row, (LANES, LANES)))
    gram = {}
    for k, (i, j) in enumerate(PAIRS):
        at = r * len(PAIRS) + k
        gram[i, j] = gram[j, i] = column[at : at + 1, 0:1]
    return gram


def basis_kernel(cities, sums_ref, mine, rank, vec_1, vec_2, vec_3, out_ref):
    chunks = rank.shape[0]
    row = jnp.sum(sums_ref[...], axis=0)[0:1, :]
    lane = lax.broadcasted_iota(jnp.int32, (1, LANES), 1)
    good = row[:, OK_ROW : OK_ROW + 1] == float(cities)
    places = rank[...]
    vecs = (None, vec_1, vec_2, vec_3)
    rows, made = {}, []
    for r in range(2):
        _, residuals, fine = iterated(gram_of(row, r))
        good = good & fine
        for k, weights in enumerate(residuals):
            values = mine[(2 + r) * chunks : (3 + r) * chunks, :]
            for j in range(1, k + 2):
                values = values + weights[j] * vecs[j][r * chunks : (r + 1) * chunks, :]
                made.append(weights[j])
            rows[k, r] = taken(values, places)
    row = jnp.where(lane == OK_ROW, jnp.where(good, 1.0, 0.0), row)
    for k, value in enumerate(made):
        row = jnp.where(lane == MADE + k, value, row)
    high = row.astype(jnp.bfloat16).astype(jnp.float32)
    middle = (row - high).astype(jnp.bfloat16).astype(jnp.float32)
    low = row - high - middle
    parts = [rows[k, r] for k in range(ITERS) for r in range(2)]
    parts += [high, middle, low, jnp.zeros((SUM_ROWS - 3, LANES), jnp.float32)]
    out_ref[...] = jnp.concatenate(parts, axis=0).astype(jnp.bfloat16)


def home_kernel(info, back_ref, sums_ref, packed, field_ref, residual_ref, ok_ref):
    chunks = field_ref.shape[1] // LANES
    near, groups = sums_ref.shape[:2]
    tiles = near * groups
    terms = sums_ref[...].astype(jnp.float32).reshape(tiles, SUM_ROWS, LANES)
    terms = terms[:, 0, :] + terms[:, 1, :] + terms[:, 2, :]
    row = jnp.sum(terms, axis=0, keepdims=True)
    slot = info[1] % near * groups + info[1] // near
    here = lax.broadcasted_iota(jnp.int32, (tiles, 1), 0) == slot
    good = row[:, OK_ROW : OK_ROW + 1] == float(tiles)
    values = back_ref[0, 0].astype(jnp.float32)
    start = packed[...].astype(jnp.float32)
    count = len(PAIRS) - ITERS - 1
    for r in range(2):
        field, residuals, fine = iterated(gram_of(row, r))
        good = good & fine
        made, at = {}, MADE + r * count
        for k in range(1, ITERS + 1):
            made[k, 0] = 1.0
            for j in range(1, k + 1):
                made[k, j] = terms[:, at : at + 1]
                at += 1
        for ref, weights in ((field_ref, field), (residual_ref, residuals[-1])):
            left = dict(weights)
            result = None
            for k in range(ITERS, 0, -1):
                if k not in left:
                    continue
                share = left[k] / made[k, k]
                for j in range(k):
                    left[j] = left[j] - share * made[k, j]
                if ref is residual_ref:
                    fine = jnp.min(jnp.where(jnp.abs(share) <= MOST, 1.0, 0.0), keepdims=True)
                    good = good & (fine > 0.0)
                weight = jnp.sum(jnp.where(here, share, 0.0), axis=0, keepdims=True)
                place = (2 * (k - 1) + r) * chunks
                term = weight * values[place : place + chunks, :]
                result = term if result is None else result + term
            weight = jnp.sum(jnp.where(here, left[0], 0.0), axis=0, keepdims=True)
            result = result + weight * start[r * chunks : (r + 1) * chunks, :]
            for c in range(chunks):
                ref[r : r + 1, c * LANES : (c + 1) * LANES] = result[c : c + 1, :]
    ok_ref[0] = jnp.max(jnp.where(good, 1.0, 0.0)).astype(jnp.int32)


def tile_gather(block):
    return lax.all_gather(lax.all_gather(block, "far"), "near")


def whole(shape):
    return pl.BlockSpec(shape, lambda i, *_: (0,) * len(shape))


def params(mib=16):
    return pltpu.CompilerParams(vmem_limit_bytes=mib * 1024 * 1024)


def body(right_side, noise_var, coords, counts, pair_list):
    own = lax.axis_index(TILE).astype(jnp.int32)
    tiles, cities = lax.axis_size(TILE), lax.axis_size("city")
    length = right_side.shape[1]
    chunks = length // LANES
    rows = 5 * chunks
    table = pair_list.reshape(-1)
    entries = table.shape[0]
    f32 = functools.partial(jax.ShapeDtypeStruct, dtype=jnp.float32)

    packed = pl.pallas_call(
        pack_kernel,
        grid_spec=pltpu.PrefetchScalarGridSpec(
            num_scalar_prefetch=2,
            grid=(1,),
            in_specs=[whole((2, length)), whole((1, length))],
            out_specs=whole((4 * chunks, LANES)),
        ),
        out_shape=jax.ShapeDtypeStruct((4 * chunks, LANES), jnp.bfloat16),
        compiler_params=params(),
        name="pack",
    )(counts, table, right_side, noise_var[None, :])

    gathered = tile_gather(packed)
    city_table = gathered[:, :, 3 * chunks, :entries].astype(jnp.int32).reshape(tiles, entries)
    mine, rank, info = pl.pallas_call(
        order_kernel,
        in_specs=[
            pl.BlockSpec(memory_space=SMEM),
            pl.BlockSpec(memory_space=SMEM),
            pl.BlockSpec(memory_space=pl.ANY),
            pl.BlockSpec(memory_space=pl.ANY),
        ],
        out_specs=[
            pl.BlockSpec(memory_space=VMEM),
            pl.BlockSpec(memory_space=VMEM),
            pl.BlockSpec(memory_space=SMEM),
        ],
        out_shape=[
            f32((rows, LANES)),
            jax.ShapeDtypeStruct((chunks, LANES), jnp.int32),
            jax.ShapeDtypeStruct((8,), jnp.int32),
        ],
        scratch_shapes=[
            pltpu.SMEM((2 * tiles,), jnp.int32),
            pltpu.SMEM((tiles,), jnp.int32),
            pltpu.SMEM((tiles,), jnp.int32),
            pltpu.VMEM((4 * chunks, LANES), jnp.bfloat16),
            pltpu.VMEM((2, length), jnp.float32),
            pltpu.SemaphoreType.DMA((2,)),
        ],
        compiler_params=params(),
        name="order",
    )(own[None], city_table, gathered, coords)

    forward = [(i, i + 1) for i in range(tiles * cities - 1)]
    backward = [(j, i) for i, j in forward]

    def neighbours(block):
        axes = ("city", *TILE)
        return lax.ppermute(block, axes, forward), lax.ppermute(block, axes, backward)

    in_vmem = pl.BlockSpec(memory_space=VMEM)
    in_smem = pl.BlockSpec(memory_space=SMEM)
    spread_scratch = [pltpu.VMEM((length, LANES), jnp.float32)] * 2
    before, after = neighbours(mine)
    vec_1, blocks, bounds, far = pl.pallas_call(
        build_kernel,
        in_specs=[in_smem] + [in_vmem] * 3,
        out_specs=[in_vmem, in_vmem, in_smem, in_vmem],
        out_shape=[
            f32((2 * chunks, LANES)),
            pltpu.VMEM((KEPT, LANES, 2 * LANES), jnp.bfloat16),
            jax.ShapeDtypeStruct((6 * chunks + 1,), jnp.int32),
            f32((3, 2 * chunks, LANES)),
        ],
        scratch_shapes=spread_scratch,
        compiler_params=params(),
        name="build",
    )(info, mine, before, after)
    blocks = pltpu.with_memory_space_constraint(blocks, VMEM)

    def apply(vec):
        before, after = neighbours(vec)
        return pl.pallas_call(
            apply_kernel,
            in_specs=[in_smem] + [in_vmem] * 6,
            out_specs=in_vmem,
            out_shape=f32((2 * chunks, LANES)),
            scratch_shapes=spread_scratch,
            compiler_params=params(),
            name="apply",
        )(bounds, mine, vec, before, after, far, blocks)

    vec_2 = apply(vec_1)
    vec_3 = apply(vec_2)

    sums = pl.pallas_call(
        sums_kernel,
        grid_spec=pltpu.PrefetchScalarGridSpec(
            num_scalar_prefetch=1,
            grid=(1,),
            in_specs=[whole((rows, LANES))] + [whole((2 * chunks, LANES))] * 3,
            out_specs=whole((8, LANES)),
        ),
        out_shape=f32((8, LANES)),
        compiler_params=params(),
        name="sums",
    )(info, mine, vec_1, vec_2, vec_3)
    size = 6 * chunks + SUM_ROWS
    basis = pl.pallas_call(
        functools.partial(basis_kernel, cities),
        out_shape=jax.ShapeDtypeStruct((size, LANES), jnp.bfloat16),
        compiler_params=params(),
        name="basis",
    )(lax.all_gather(sums, "city"), mine, rank, vec_1, vec_2, vec_3)
    back = tile_gather(basis)
    near, groups = back.shape[:2]
    field, residual, good = pl.pallas_call(
        home_kernel,
        grid_spec=pltpu.PrefetchScalarGridSpec(
            num_scalar_prefetch=1,
            grid=(1,),
            in_specs=[
                pl.BlockSpec(
                    (1, 1, size, LANES), lambda i, info: (info[1] % near, info[1] // near, 0, 0)
                ),
                pl.BlockSpec(
                    (near, groups, SUM_ROWS, LANES),
                    lambda i, info: (0, 0, 6 * chunks // SUM_ROWS, 0),
                ),
                whole((4 * chunks, LANES)),
            ],
            out_specs=[whole((2, length)), whole((2, length)), pl.BlockSpec(memory_space=SMEM)],
        ),
        out_shape=[f32((2, length)), f32((2, length)), jax.ShapeDtypeStruct((1,), jnp.int32)],
        compiler_params=params(),
        name="home",
    )(info, back, back, packed)
    return lax.cond(
        good[0] > 0,
        lambda *args: (field, residual),
        any_graph,
        right_side,
        noise_var,
        coords,
        counts,
        pair_list,
    )


def solution(mesh):
    cities, tiles = mesh.devices.shape
    groups = 4 if tiles % 8 == 0 else 2
    mesh = jax.sharding.Mesh(mesh.devices.reshape(cities, groups, tiles // groups), ("city", *TILE))
    placed = (
        P(None, ("city", *TILE)),
        P(("city", *TILE)),
        P(None, "city"),
        P(("city", *TILE)),
        P(("city", *TILE), None, None),
    )
    return jax.shard_map(
        body,
        mesh=mesh,
        in_specs=placed,
        out_specs=(P(None, ("city", *TILE)), P(None, ("city", *TILE))),
        check_vma=False,
    )
```
